32 devices in a mesh: tm: 8 (over z, x), rows: 4 (over y, core).
Axes of the slice: x: 2, y: 2, z: 4, core: 2. Of those that a mesh axis runs over, the one named last changes fastest.
Arguments:
- features: bfloat16 [32, 96, 16, 256], P('tm', None, 'rows'), may hold values from -6 to 6
- first_kernel: bfloat16 [3, 3, 3, 96, 96], replicated, may hold values from -0.125 to 0.125
- first_bias: float32 [96], replicated, may hold values from -3 to 3
- first_gain: float32 [96], replicated, may hold values from 0.1 to 1.9
- second_kernel: bfloat16 [3, 3, 3, 96, 96], replicated, may hold values from -0.125 to 0.125
- latent_weight: bfloat16 [4, 16, 96], replicated, may hold values from -0.3125 to 0.3125
- decode_kernel: bfloat16 [3, 3, 3, 96, 16], replicated, may hold values from -0.3125 to 0.3125
- decode_bias: float32 [96], replicated, may hold values from -3 to 3
- decode_gain: float32 [96], replicated, may hold values from 0.1 to 1.9
- upsample_weight: bfloat16 [4, 96, 96], replicated, may hold values from -0.625 to 0.625
- final_kernel: bfloat16 [3, 3, 3, 96, 96], replicated, may hold values from -0.125 to 0.125
Outputs:
- latents: bfloat16 [8, 16, 16, 256], P('tm', None, 'rows')
- rebuilt: bfloat16 [32, 96, 16, 256], P('tm', None, 'rows')
The draws below stay inside these ranges and needn't reach their ends.
All inputs are finite; a program needn't handle non-finite values.
Results may differ from the reference program's by a relative error of at most 0.01.
Values may be sent and summed in bfloat16 or wider, within the bound.
A program may use at most 64 MiB of HBM per device.

```python
import jax
import jax.numpy as jnp
from jax import lax

C = 96
Z = 16
SPAN = 4
COLS = 256
FRAMES = 32
LATENTS = 8
ROWS = 16


def steps_of(own_key, shape, shards, least, top_value):
    loudness, own = 1.0, jax.random.fold_in(own_key, 6)
    for position, parts in shards:
        heights = jnp.exp(jax.random.uniform(jax.random.fold_in(own, position), (parts,), jnp.float32, least / len(shards), top_value / len(shards)))
        loudness = loudness * jnp.repeat(heights, shape[position] // parts).reshape([-1 if axis == position else 1 for axis in range(len(shape))])
    return loudness


def bell_draw(own_key, shape, width, reach, split=(), held_as=jnp.bfloat16):
    drawn = width * jax.random.normal(own_key, shape, jnp.float32)
    if split:
        drawn = drawn * steps_of(own_key, shape, split, -0.22, 0.18)
    return jnp.clip(drawn, -reach, reach).astype(held_as)


def setup_inputs(seed: int = 0) -> dict:
    seeds = jax.random.split(jax.random.key(seed), 12)
    return {
        "features": bell_draw(seeds[0], (FRAMES, C, ROWS, COLS), 1.0, 6.0, ((0, 8), (2, 4))),
        "first_kernel": bell_draw(seeds[1], (3, 3, 3, C, C), (27 * C) ** -0.5, 0.125),
        "first_bias": bell_draw(seeds[2], (C,), 0.5, 3.0, (), jnp.float32),
        "first_gain": jnp.clip(1.0 + 0.18 * jax.random.normal(seeds[3], (C,), jnp.float32), 0.1, 1.9),
        "second_kernel": bell_draw(seeds[4], (3, 3, 3, C, C), (27 * C) ** -0.5, 0.125),
        "latent_weight": bell_draw(seeds[5], (SPAN, Z, C), (SPAN * C) ** -0.5, 0.3125),
        "decode_kernel": bell_draw(seeds[6], (3, 3, 3, C, Z), (27 * Z) ** -0.5, 0.3125),
        "decode_bias": bell_draw(seeds[7], (C,), 0.5, 3.0, (), jnp.float32),
        "decode_gain": jnp.clip(1.0 + 0.18 * jax.random.normal(seeds[8], (C,), jnp.float32), 0.1, 1.9),
        "upsample_weight": bell_draw(seeds[9], (SPAN, C, C), C ** -0.5, 0.625),
        "final_kernel": bell_draw(seeds[10], (3, 3, 3, C, C), (27 * C) ** -0.5, 0.125),
    }


def causal_conv(values, kernel):
    left_side = values.astype(jnp.float32).transpose(1, 0, 2, 3)[None]
    right_side = kernel.astype(jnp.float32).transpose(3, 4, 0, 1, 2)
    result = lax.conv_general_dilated(left_side, right_side, (1, 1, 1), [(2, 0), (1, 1), (1, 1)], dimension_numbers=('NCDHW', 'OIDHW', 'NCDHW'), precision=lax.Precision.HIGHEST)
    return result[0].transpose(1, 0, 2, 3)

def normed_silu(values, gain):
    scale = lax.rsqrt(lax.optimization_barrier(jnp.mean(values * values, axis=1, keepdims=True)) + 1e-06)
    return jax.nn.silu(values * scale * gain.astype(jnp.float32)[None, :, None, None])

def reference(features, first_kernel, first_bias, first_gain, second_kernel, latent_weight, decode_kernel, decode_bias, decode_gain, upsample_weight, final_kernel):
    first = causal_conv(features, first_kernel) + first_bias.astype(jnp.float32)[None, :, None, None]
    gated = normed_silu(first, first_gain).astype(jnp.bfloat16)
    hidden = (features.astype(jnp.float32) + causal_conv(gated, second_kernel)).astype(jnp.bfloat16)
    grouped = hidden.astype(jnp.float32).reshape(LATENTS, SPAN, C, ROWS, COLS)
    latents = jnp.einsum('jzc,kjcrw->kzrw', latent_weight.astype(jnp.float32), grouped, precision=lax.Precision.HIGHEST).astype(jnp.bfloat16)
    decoded = causal_conv(latents, decode_kernel) + decode_bias.astype(jnp.float32)[None, :, None, None]
    activated = normed_silu(decoded, decode_gain).astype(jnp.bfloat16)
    upsampled = jnp.einsum('joc,kcrw->kjorw', upsample_weight.astype(jnp.float32), activated.astype(jnp.float32), precision=lax.Precision.HIGHEST)
    upsampled = upsampled.reshape(FRAMES, C, ROWS, COLS).astype(jnp.bfloat16)
    rebuilt = (upsampled.astype(jnp.float32) + causal_conv(upsampled, final_kernel)).astype(jnp.bfloat16)
    return (latents, rebuilt)
```

```python
import functools

import jax
import jax.numpy as jnp
from jax import lax
from jax.experimental import pallas as pl
from jax.experimental.pallas import tpu as pltpu
from jax.sharding import PartitionSpec as P

F32 = jnp.float32
BF16 = jnp.bfloat16
MESH = pl.DeviceIdType.MESH


def dot(a, b):
    return jnp.dot(a, b, preferred_element_type=F32)


def col_taps(x):
    w = x.shape[1]
    lane = lax.broadcasted_iota(jnp.int32, x.shape, 1)
    left = jnp.where(lane == 0, 0.0, pltpu.roll(x, 1, 1))
    right = jnp.where(lane == w - 1, 0.0, pltpu.roll(x, w - 1, 1))
    return left.astype(BF16), x.astype(BF16), right.astype(BF16)


def norm_silu(v, gain):
    scale = lax.rsqrt(jnp.mean(v * v, axis=0, keepdims=True) + 1e-6)
    u = v * scale * gain
    return u / (1.0 + jnp.exp(-u))


def kernel(
    spans,
    bands,
    x_ref,
    k1_ref,
    b1_ref,
    g1_ref,
    k2_ref,
    wl_ref,
    wd_ref,
    bd_ref,
    gd_ref,
    up_ref,
    k3_ref,
    lat_ref,
    out_ref,
    rx_t,
    rx_r,
    xs,
    acc,
    w1,
    v2,
    w3,
    la,
    ln,
    rxm,
    rxs,
    lr,
    ls,
    act,
    s_feat,
    r_feat,
    s_part,
    r_part,
    s_lat,
    r_lat,
):
    C = x_ref.shape[2]
    W = x_ref.shape[3]
    Z = wl_ref.shape[1]
    R = x_ref.shape[1]
    tm = lax.axis_index("tm")
    rb = lax.axis_index("rows")
    has_next = tm < spans - 1
    has_prev = tm > 0
    up_ok = rb > 0
    dn_ok = rb < bands - 1
    side_ok = {-1: up_ok, 0: None, 1: dn_ok}

    def both(*conds):
        out = None
        for c in conds:
            if c is None:
                continue
            out = c if out is None else jnp.logical_and(out, c)
        return out

    def when(cond, fn):
        if cond is None:
            fn()
        else:
            pl.when(cond)(fn)

    barrier = pltpu.get_barrier_semaphore()
    expect = jnp.int32(0)
    for d in range(4):
        for s in (-1, 0, 1):
            if d == 0 and s == 0:
                continue

            def greet(d=d, s=s):
                pl.semaphore_signal(
                    barrier, inc=1, device_id=(tm - d, rb + s), device_id_type=MESH
                )

            when(both(tm >= d, side_ok[s]) if d else side_ok[s], greet)
            ok = both(tm < spans - d, side_ok[s])
            expect = expect + jnp.where(ok, 1, 0)
    pl.semaphore_wait(barrier, expect)

    def copy(src, dst, ssem, rsem, d, s):
        return pltpu.make_async_remote_copy(
            src_ref=src,
            dst_ref=dst,
            send_sem=ssem,
            recv_sem=rsem,
            device_id=(tm + d, rb + s),
            device_id_type=MESH,
        )

    own_up = copy(x_ref.at[:, 0], rx_r.at[1, pl.ds(2, 4)], s_feat.at[0], r_feat.at[0], 0, -1)
    own_dn = copy(x_ref.at[:, R - 1], rx_r.at[0, pl.ds(2, 4)], s_feat.at[1], r_feat.at[1], 0, 1)
    ahead = copy(x_ref.at[pl.ds(2, 2)], rx_t, s_feat.at[2], r_feat.at[2], 1, 0)
    fwd_up = copy(rx_t.at[:, 0], rx_r.at[1, pl.ds(0, 2)], s_feat.at[3], r_feat.at[3], 0, -1)
    fwd_dn = copy(rx_t.at[:, R - 1], rx_r.at[0, pl.ds(0, 2)], s_feat.at[4], r_feat.at[4], 0, 1)
    when(has_next, ahead.start)
    when(up_ok, own_up.start)
    when(dn_ok, own_dn.start)

    def zero(ref, idx):
        def go():
            ref[idx] = jnp.zeros(ref[idx].shape, ref.dtype)

        return go

    when(jnp.logical_not(up_ok), zero(rx_r, (0,)))
    when(jnp.logical_not(dn_ok), zero(rx_r, (1,)))

    for a in range(3):
        w1[a * C : (a + 1) * C, :] = jnp.concatenate(
            [k1_ref[a * 9 + be] for be in range(9)], axis=1
        )

    def put_stack(ref, f, row, x):
        for e, part in enumerate(col_taps(x)):
            ref[f, row, e * C : (e + 1) * C, :] = part

    def own_rows(i, _):
        f, r = i // R, i % R
        put_stack(xs, f + 2, r + 1, x_ref[f, r].astype(F32))
        return 0

    lax.fori_loop(0, 4 * R, own_rows, 0)

    wl = jnp.concatenate([wl_ref[j] for j in range(4)], axis=0)
    for b in range(3):
        g = [[dot(wl, k2_ref[a * 9 + b * 3 + e]) for e in range(3)] for a in range(3)]
        for f in range(4):
            rows = []
            own = [(j, f - j + 2) for j in range(4) if 0 <= f - j + 2 <= 2]
            nxt = [(j, f - 2 - j) for j in range(4) if 0 <= f - 2 - j <= 2]
            for terms in (own, nxt):
                if not terms:
                    continue
                rows.append(
                    jnp.concatenate(
                        [sum(g[a][e][j * Z : (j + 1) * Z] for j, a in terms) for e in range(3)],
                        axis=1,
                    ).astype(BF16)
                )
            n = len(rows)
            for i in range(n):
                v2[f, (b * n + i) * Z : (b * n + i + 1) * Z, :] = rows[i]

    when(dn_ok, own_up.wait_recv)
    when(up_ok, own_dn.wait_recv)

    def halo_rows(first):
        def go(f, _):
            put_stack(xs, f, 0, rx_r[0, f].astype(F32))
            put_stack(xs, f, R + 1, rx_r[1, f].astype(F32))
            return 0

        return go

    lax.fori_loop(2, 6, halo_rows(2), 0)
    b1 = b1_ref[...]
    g1 = g1_ref[...]

    def window(f, r):
        return jnp.concatenate([xs[f, r], xs[f, r + 1], xs[f, r + 2]], axis=0)

    def conv_own(r, _):
        for fi in range(2, 6):
            lo, hi = max(0, fi - 3), min(2, fi)
            y = dot(w1[lo * C : (hi + 1) * C, :], window(fi, r))
            for a in range(lo, hi + 1):
                t = fi - a
                part = y[(a - lo) * C : (a - lo + 1) * C]
                if (fi == 2) or (fi == 3 and t == 3):
                    acc[t, r] = part + b1
                else:
                    acc[t, r] += part
        return 0

    lax.fori_loop(0, R, conv_own, 0)

    la[...] = jnp.zeros(la.shape, F32)
    ln[...] = jnp.zeros(ln.shape, F32)

    def gate(t):
        def go(r, _):
            gated = norm_silu(acc[t, r], g1)
            stack = jnp.concatenate(col_taps(gated), axis=0)
            n = 2 if t >= 2 else 1
            y = dot(v2[t, : 3 * n * Z, :], stack)
            for b in range(3):
                la[r - b + 2] += y[b * n * Z : (b * n + 1) * Z]
                if n == 2:
                    ln[r - b + 2] += y[(b * n + 1) * Z : (b * n + 2) * Z]
            la[r + 1] += dot(wl_ref[t], x_ref[t, r])
            return 0

        lax.fori_loop(0, R, go, 0)

    gate(2)
    gate(3)

    nx_mid = copy(ln.at[pl.ds(1, R)], rxm, s_part.at[0], r_part.at[0], 1, 0)
    nx_up = copy(ln.at[0], rxs.at[2], s_part.at[1], r_part.at[1], 1, -1)
    nx_dn = copy(ln.at[R + 1], rxs.at[3], s_part.at[2], r_part.at[2], 1, 1)
    when(has_next, nx_mid.start)
    when(both(has_next, up_ok), nx_up.start)
    when(both(has_next, dn_ok), nx_dn.start)

    when(has_prev, ahead.wait_recv)
    when(both(has_prev, up_ok), fwd_up.start)
    when(both(has_prev, dn_ok), fwd_dn.start)

    def no_prev():
        rx_t[...] = jnp.zeros(rx_t.shape, BF16)
        rx_r[0, 0:2] = jnp.zeros((2, C, W), BF16)
        rx_r[1, 0:2] = jnp.zeros((2, C, W), BF16)

    when(jnp.logical_not(has_prev), no_prev)

    ups = [up_ref[j] for j in range(4)]
    for be in range(9):
        k3 = jnp.concatenate([k3_ref[a * 9 + be] for a in range(3)], axis=0)
        f3 = [dot(k3, ups[j]) for j in range(4)]
        for j in range(4):
            total = sum(f3[j + a - 2][a * C : (a + 1) * C] for a in range(3) if j + a >= 2)
            if be == 4:
                total = total + ups[j].astype(F32)
            w3[j * C : (j + 1) * C, be * C : (be + 1) * C] = total.astype(BF16)
        for j in range(2):
            total = sum(f3[j + a + 2][a * C : (a + 1) * C] for a in range(3) if j + a < 2)
            w3[(4 + j) * C : (5 + j) * C, be * C : (be + 1) * C] = total.astype(BF16)

    def prev_rows(i, _):
        f, r = i // R, i % R
        put_stack(xs, f, r + 1, rx_t[f, r].astype(F32))
        return 0

    lax.fori_loop(0, 2 * R, prev_rows, 0)
    when(both(has_prev, dn_ok), fwd_up.wait_recv)
    when(both(has_prev, up_ok), fwd_dn.wait_recv)
    lax.fori_loop(0, 2, halo_rows(0), 0)

    def conv_prev(r, _):
        y = dot(w1[: 2 * C, :], window(1, r))
        acc[1, r] += y[:C]
        acc[0, r] += y[C:] + dot(w1[:C, :], window(0, r))
        return 0

    lax.fori_loop(0, R, conv_prev, 0)
    gate(0)
    gate(1)

    ow_up = copy(la.at[0], rxs.at[0], s_part.at[3], r_part.at[3], 0, -1)
    ow_dn = copy(la.at[R + 1], rxs.at[1], s_part.at[4], r_part.at[4], 0, 1)
    when(up_ok, ow_up.start)
    when(dn_ok, ow_dn.start)

    no = jnp.logical_not
    when(no(has_prev), zero(rxm, (slice(None),)))
    when(no(dn_ok), zero(rxs, (0,)))
    when(no(up_ok), zero(rxs, (1,)))
    when(no(both(has_prev, dn_ok)), zero(rxs, (2,)))
    when(no(both(has_prev, up_ok)), zero(rxs, (3,)))
    when(has_prev, nx_mid.wait_recv)
    when(both(has_prev, dn_ok), nx_up.wait_recv)
    when(both(has_prev, up_ok), nx_dn.wait_recv)
    when(dn_ok, ow_up.wait_recv)
    when(up_ok, ow_dn.wait_recv)
    for r in range(R):
        total = la[r + 1] + rxm[r]
        if r == 0:
            total = total + rxs[1] + rxs[3]
        if r == R - 1:
            total = total + rxs[0] + rxs[2]
        lr[3, r + 2] = total.astype(BF16)

    sends = []
    for d in range(4):
        for s in (0, -1, 1):
            if d == 0 and s == 0:
                continue
            src = {0: pl.ds(2, R), -1: pl.ds(2, 2), 1: pl.ds(R, 2)}[s]
            dst = {0: pl.ds(2, R), -1: pl.ds(R + 2, 2), 1: pl.ds(0, 2)}[s]
            c = copy(
                lr.at[3, src], lr.at[3 - d, dst], s_lat.at[d, s + 1], r_lat.at[d, s + 1], d, s
            )
            when(both(tm < spans - d if d else None, side_ok[s]), c.start)
            sends.append((d, s, c))
    lat_ref[...] = lr[3, 2 : R + 2]
    for d, s, c in sends:
        dst = {0: slice(2, R + 2), -1: slice(R + 2, R + 4), 1: slice(0, 2)}[s]
        ok = both(tm >= d if d else None, side_ok[-s])
        when(no(ok), zero(lr, (3 - d, dst)))
        when(ok, c.wait_recv)

    def lat_rows(row, _):
        for f in range(4):
            for e, part in enumerate(col_taps(lr[f, row].astype(F32))):
                ls[row, (f * 3 + e) * Z : (f * 3 + e + 1) * Z, :] = part
        return 0

    lax.fori_loop(0, R + 4, lat_rows, 0)
    bd = bd_ref[...]
    gd = gd_ref[...]
    prev_on = jnp.where(has_prev, 1.0, 0.0)

    def decode(row, _):
        k = jnp.concatenate([ls[row], ls[row + 1], ls[row + 2]], axis=0)
        y = dot(wd_ref[...], k)
        grow = rb * R + row - 1
        on = jnp.where(jnp.logical_and(grow >= 0, grow < bands * R), 1.0, 0.0)
        put_stack(act, 0, row, norm_silu(y[:C] + bd, gd) * (on * prev_on))
        put_stack(act, 1, row, norm_silu(y[C:] + bd, gd) * on)
        return 0

    lax.fori_loop(0, R + 2, decode, 0)

    def finish(r, _):
        cur = jnp.concatenate([act[1, r], act[1, r + 1], act[1, r + 2]], axis=0)
        old = jnp.concatenate([act[0, r], act[0, r + 1], act[0, r + 2]], axis=0)
        y = dot(w3[: 4 * C, :], cur)
        z = dot(w3[4 * C :, :], old)
        for j in range(4):
            part = y[j * C : (j + 1) * C]
            if j < 2:
                part = part + z[j * C : (j + 1) * C]
            out_ref[j, r] = part.astype(BF16)
        return 0

    lax.fori_loop(0, R, finish, 0)

    when(up_ok, own_up.wait_send)
    when(dn_ok, own_dn.wait_send)
    when(has_next, ahead.wait_send)
    when(both(has_prev, up_ok), fwd_up.wait_send)
    when(both(has_prev, dn_ok), fwd_dn.wait_send)
    when(has_next, nx_mid.wait_send)
    when(both(has_next, up_ok), nx_up.wait_send)
    when(both(has_next, dn_ok), nx_dn.wait_send)
    when(up_ok, ow_up.wait_send)
    when(dn_ok, ow_dn.wait_send)
    for d, s, c in sends:
        when(both(tm < spans - d if d else None, side_ok[s]), c.wait_send)


def body(
    spans,
    bands,
    features,
    first_kernel,
    first_bias,
    first_gain,
    second_kernel,
    latent_weight,
    decode_kernel,
    decode_bias,
    decode_gain,
    upsample_weight,
    final_kernel,
):
    T, C, R, W = features.shape
    Z = latent_weight.shape[1]
    x = features.transpose(0, 2, 1, 3)
    dk = decode_kernel.transpose(3, 1, 0, 2, 4).reshape(C, 3, 3, 3 * Z)
    wd = jnp.concatenate(
        [
            jnp.pad(dk, ((0, 0), (0, 0), (0, 1), (0, 0))).reshape(C, 36 * Z),
            jnp.pad(dk, ((0, 0), (0, 0), (1, 0), (0, 0))).reshape(C, 36 * Z),
        ],
        0,
    )
    vmem = pl.BlockSpec(memory_space=pltpu.VMEM)
    lat, out = pl.pallas_call(
        functools.partial(kernel, spans, bands),
        out_shape=(
            jax.ShapeDtypeStruct((R, Z, W), BF16),
            jax.ShapeDtypeStruct((T, R, C, W), BF16),
        ),
        in_specs=[vmem] * 11,
        out_specs=(vmem, vmem),
        scratch_shapes=[
            pltpu.VMEM((2, R, C, W), BF16),
            pltpu.VMEM((2, 6, C, W), BF16),
            pltpu.VMEM((6, R + 2, 3 * C, W), BF16),
            pltpu.VMEM((4, R, C, W), F32),
            pltpu.VMEM((3 * C, 9 * C), BF16),
            pltpu.VMEM((4, 6 * Z, 3 * C), BF16),
            pltpu.VMEM((6 * C, 9 * C), BF16),
            pltpu.VMEM((R + 2, Z, W), F32),
            pltpu.VMEM((R + 2, Z, W), F32),
            pltpu.VMEM((R, Z, W), F32),
            pltpu.VMEM((4, Z, W), F32),
            pltpu.VMEM((4, R + 4, Z, W), BF16),
            pltpu.VMEM((R + 4, 12 * Z, W), BF16),
            pltpu.VMEM((2, R + 2, 3 * C, W), BF16),
            pltpu.SemaphoreType.DMA((5,)),
            pltpu.SemaphoreType.DMA((5,)),
            pltpu.SemaphoreType.DMA((5,)),
            pltpu.SemaphoreType.DMA((5,)),
            pltpu.SemaphoreType.DMA((4, 3)),
            pltpu.SemaphoreType.DMA((4, 3)),
        ],
        compiler_params=pltpu.CompilerParams(
            collective_id=0, has_side_effects=True, vmem_limit_bytes=48 * 1024 * 1024
        ),
    )(
        x,
        first_kernel.reshape(27, C, C),
        first_bias.reshape(C, 1),
        first_gain.reshape(C, 1),
        second_kernel.reshape(27, C, C),
        latent_weight,
        wd,
        decode_bias.reshape(C, 1),
        decode_gain.reshape(C, 1),
        upsample_weight,
        final_kernel.reshape(27, C, C),
    )
    return lat.transpose(1, 0, 2)[None], out.transpose(0, 2, 1, 3)


def solution(mesh):
    spans = mesh.shape["tm"]
    bands = mesh.shape["rows"]
    return jax.shard_map(
        functools.partial(body, spans, bands),
        mesh=mesh,
        in_specs=(P("tm", None, "rows", None),) + (P(),) * 10,
        out_specs=(P("tm", None, "rows", None), P("tm", None, "rows", None)),
        check_vma=False,
    )
```

```python
import functools

import jax
import jax.numpy as jnp
from jax import lax
from jax.experimental import pallas as pl
from jax.experimental.pallas import tpu as pltpu
from jax.sharding import PartitionSpec as P

F32 = jnp.float32
BF16 = jnp.bfloat16
MESH = pl.DeviceIdType.MESH


def dot(a, b):
    return jnp.dot(a, b, preferred_element_type=F32)


def col_taps(x):
    w = x.shape[1]
    lane = lax.broadcasted_iota(jnp.int32, x.shape, 1)
    left = jnp.where(lane == 0, 0.0, pltpu.roll(x, 1, 1))
    right = jnp.where(lane == w - 1, 0.0, pltpu.roll(x, w - 1, 1))
    return left.astype(BF16), x.astype(BF16), right.astype(BF16)


def norm_silu(v, gain):
    scale = lax.rsqrt(jnp.mean(v * v, axis=0, keepdims=True) + 1e-6)
    u = v * scale * gain
    return u / (1.0 + jnp.exp(-u))


def kernel(
    spans,
    bands,
    x_ref,
    b1_ref,
    g1_ref,
    bd_ref,
    gd_ref,
    k1_hbm,
    k2_hbm,
    wl_hbm,
    dk_hbm,
    up_hbm,
    k3_hbm,
    lat_ref,
    out_ref,
    rx_t,
    rx_r,
    xs,
    acc,
    w1,
    v2,
    w3,
    la,
    ln,
    rxm,
    rxs,
    lr,
    ls,
    act,
    k1_ref,
    k2_ref,
    wl_ref,
    dk_ref,
    up_ref,
    k3_ref,
    wd_ref,
    s_load,
    s_feat,
    r_feat,
    s_part,
    r_part,
    s_lat,
    r_lat,
):
    C = x_ref.shape[2]
    W = x_ref.shape[3]
    Z = wl_ref.shape[1]
    R = x_ref.shape[1]
    tm = lax.axis_index("tm")
    rb = lax.axis_index("rows")
    has_next = tm < spans - 1
    has_prev = tm > 0
    up_ok = rb > 0
    dn_ok = rb < bands - 1
    side_ok = {-1: up_ok, 0: None, 1: dn_ok}

    def both(*conds):
        out = None
        for c in conds:
            if c is None:
                continue
            out = c if out is None else jnp.logical_and(out, c)
        return out

    def when(cond, fn):
        if cond is None:
            fn()
        else:
            pl.when(cond)(fn)

    barrier = pltpu.get_barrier_semaphore()
    expect = jnp.int32(0)
    for d in range(4):
        for s in (-1, 0, 1):
            if d == 0 and s == 0:
                continue

            def greet(d=d, s=s):
                pl.semaphore_signal(
                    barrier, inc=1, device_id=(tm - d, rb + s), device_id_type=MESH
                )

            when(both(tm >= d, side_ok[s]) if d else side_ok[s], greet)
            ok = both(tm < spans - d, side_ok[s])
            expect = expect + jnp.where(ok, 1, 0)

    loads = [
        pltpu.make_async_copy(src, dst, s_load.at[i])
        for i, (src, dst) in enumerate(
            [
                (k1_hbm, k1_ref),
                (k2_hbm, k2_ref),
                (wl_hbm, wl_ref),
                (k3_hbm, k3_ref),
                (up_hbm, up_ref),
                (dk_hbm, dk_ref),
            ]
        )
    ]
    for load in loads:
        load.start()
    pl.semaphore_wait(barrier, expect)

    def copy(src, dst, ssem, rsem, d, s):
        return pltpu.make_async_remote_copy(
            src_ref=src,
            dst_ref=dst,
            send_sem=ssem,
            recv_sem=rsem,
            device_id=(tm + d, rb + s),
            device_id_type=MESH,
        )

    own_up = copy(x_ref.at[:, 0], rx_r.at[1, pl.ds(2, 4)], s_feat.at[0], r_feat.at[0], 0, -1)
    own_dn = copy(x_ref.at[:, R - 1], rx_r.at[0, pl.ds(2, 4)], s_feat.at[1], r_feat.at[1], 0, 1)
    pieces = [(1, 0, 1), (1, R - 1, 1), (1, 1, R - 2), (0, 0, 1), (0, R - 1, 1), (0, 1, R - 2)]
    ahead = [
        copy(
            x_ref.at[2 + f, pl.ds(r, n)],
            rx_t.at[f, pl.ds(r, n)],
            s_feat.at[2 + i],
            r_feat.at[2 + i],
            1,
            0,
        )
        for i, (f, r, n) in enumerate(pieces)
    ]
    fwd_up = [
        copy(rx_t.at[f, 0], rx_r.at[1, f], s_feat.at[8 + f], r_feat.at[8 + f], 0, -1)
        for f in range(2)
    ]
    fwd_dn = [
        copy(rx_t.at[f, R - 1], rx_r.at[0, f], s_feat.at[10 + f], r_feat.at[10 + f], 0, 1)
        for f in range(2)
    ]
    for c in ahead:
        when(has_next, c.start)
    when(up_ok, own_up.start)
    when(dn_ok, own_dn.start)

    def zero(ref, idx):
        def go():
            ref[idx] = jnp.zeros(ref[idx].shape, ref.dtype)

        return go

    when(jnp.logical_not(up_ok), zero(rx_r, (0,)))
    when(jnp.logical_not(dn_ok), zero(rx_r, (1,)))

    def column(ref):
        c = ref.shape[1]
        i = lax.broadcasted_iota(jnp.int32, (c, c), 0)
        j = lax.broadcasted_iota(jnp.int32, (c, c), 1)
        return jnp.sum(jnp.where(i == j, ref[...], 0.0), axis=1, keepdims=True)

    loads[0].wait()
    for a in range(3):
        w1[a * C : (a + 1) * C, :] = jnp.concatenate(
            [k1_ref[a * 9 + be] for be in range(9)], axis=1
        )

    def put_stack(ref, f, row, x):
        for e, part in enumerate(col_taps(x)):
            ref[f, row, e * C : (e + 1) * C, :] = part

    def own_rows(i, _):
        f, r = i // R, i % R
        put_stack(xs, f + 2, r + 1, x_ref[f, r].astype(F32))
        return 0

    lax.fori_loop(0, 4 * R, own_rows, 0, unroll=True)

    loads[1].wait()
    loads[2].wait()
    wl = jnp.concatenate([wl_ref[j] for j in range(4)], axis=0)
    for b in range(3):
        g = [[dot(wl, k2_ref[a * 9 + b * 3 + e]) for e in range(3)] for a in range(3)]
        for f in range(4):
            rows = []
            own = [(j, f - j + 2) for j in range(4) if 0 <= f - j + 2 <= 2]
            nxt = [(j, f - 2 - j) for j in range(4) if 0 <= f - 2 - j <= 2]
            for terms in (own, nxt):
                if not terms:
                    continue
                rows.append(
                    jnp.concatenate(
                        [sum(g[a][e][j * Z : (j + 1) * Z] for j, a in terms) for e in range(3)],
                        axis=1,
                    ).astype(BF16)
                )
            n = len(rows)
            for i in range(n):
                v2[f, (b * n + i) * Z : (b * n + i + 1) * Z, :] = rows[i]

    when(dn_ok, own_up.wait_recv)
    when(up_ok, own_dn.wait_recv)

    def halo_rows(first):
        def go(f, _):
            put_stack(xs, f, 0, rx_r[0, f].astype(F32))
            put_stack(xs, f, R + 1, rx_r[1, f].astype(F32))
            return 0

        return go

    lax.fori_loop(2, 6, halo_rows(2), 0, unroll=True)
    b1 = column(b1_ref)
    g1 = column(g1_ref)

    def window(f, r):
        return jnp.concatenate([xs[f, r], xs[f, r + 1], xs[f, r + 2]], axis=0)

    def conv_own(r, _):
        for fi in range(2, 6):
            lo, hi = max(0, fi - 3), min(2, fi)
            y = dot(w1[lo * C : (hi + 1) * C, :], window(fi, r))
            for a in range(lo, hi + 1):
                t = fi - a
                part = y[(a - lo) * C : (a - lo + 1) * C]
                if (fi == 2) or (fi == 3 and t == 3):
                    acc[t, r] = part + b1
                else:
                    acc[t, r] += part
        return 0

    lax.fori_loop(0, R, conv_own, 0, unroll=True)

    la[...] = jnp.zeros(la.shape, F32)
    ln[...] = jnp.zeros(ln.shape, F32)

    def gate(t):
        def go(r, _):
            gated = norm_silu(acc[t, r], g1)
            stack = jnp.concatenate(col_taps(gated), axis=0)
            n = 2 if t >= 2 else 1
            y = dot(v2[t, : 3 * n * Z, :], stack)
            for b in range(3):
                la[r - b + 2] += y[b * n * Z : (b * n + 1) * Z]
                if n == 2:
                    ln[r - b + 2] += y[(b * n + 1) * Z : (b * n + 2) * Z]
            la[r + 1] += dot(wl_ref[t], x_ref[t, r])
            return 0

        lax.fori_loop(0, R, go, 0, unroll=True)

    gate(2)
    gate(3)

    nx_mid = copy(ln.at[pl.ds(1, R)], rxm, s_part.at[0], r_part.at[0], 1, 0)
    nx_up = copy(ln.at[0], rxs.at[2], s_part.at[1], r_part.at[1], 1, -1)
    nx_dn = copy(ln.at[R + 1], rxs.at[3], s_part.at[2], r_part.at[2], 1, 1)
    when(has_next, nx_mid.start)
    when(both(has_next, up_ok), nx_up.start)
    when(both(has_next, dn_ok), nx_dn.start)

    def no_prev():
        rx_t[...] = jnp.zeros(rx_t.shape, BF16)
        rx_r[0, 0:2] = jnp.zeros((2, C, W), BF16)
        rx_r[1, 0:2] = jnp.zeros((2, C, W), BF16)

    when(jnp.logical_not(has_prev), no_prev)

    def forward(f):
        base = 0 if f == 1 else 3
        when(has_prev, ahead[base].wait_recv)
        when(both(has_prev, up_ok), fwd_up[f].start)
        when(has_prev, ahead[base + 1].wait_recv)
        when(both(has_prev, dn_ok), fwd_dn[f].start)

    forward(1)
    loads[3].wait()
    loads[4].wait()
    loads[5].wait()
    taps = []
    for b in range(3):
        for f in range(4):
            for e in range(3):
                taps.append((f, b * 3 + e))
    none = jnp.zeros((Z, C), BF16)
    wd_ref[:C, :] = jnp.transpose(
        jnp.concatenate([dk_ref[f * 9 + be] if f < 3 else none for f, be in taps], axis=0)
    )
    wd_ref[C:, :] = jnp.transpose(
        jnp.concatenate([dk_ref[(f - 1) * 9 + be] if f > 0 else none for f, be in taps], axis=0)
    )

    ups = [up_ref[j] for j in range(4)]
    for be in range(9):
        k3 = jnp.concatenate([k3_ref[a * 9 + be] for a in range(3)], axis=0)
        f3 = [dot(k3, ups[j]) for j in range(4)]
        for j in range(4):
            total = sum(f3[j + a - 2][a * C : (a + 1) * C] for a in range(3) if j + a >= 2)
            if be == 4:
                total = total + ups[j].astype(F32)
            w3[j * C : (j + 1) * C, be * C : (be + 1) * C] = total.astype(BF16)
        for j in range(2):
            total = sum(f3[j + a + 2][a * C : (a + 1) * C] for a in range(3) if j + a < 2)
            w3[(4 + j) * C : (5 + j) * C, be * C : (be + 1) * C] = total.astype(BF16)

    def prev_frame(f):
        when(has_prev, ahead[2 if f == 1 else 5].wait_recv)
        for r in range(R):
            put_stack(xs, f, r + 1, rx_t[f, r].astype(F32))
        when(both(has_prev, dn_ok), fwd_up[f].wait_recv)
        when(both(has_prev, up_ok), fwd_dn[f].wait_recv)
        put_stack(xs, f, 0, rx_r[0, f].astype(F32))
        put_stack(xs, f, R + 1, rx_r[1, f].astype(F32))

    prev_frame(1)
    for r in range(R):
        y = dot(w1[: 2 * C, :], window(1, r))
        acc[1, r] += y[:C]
        acc[0, r] += y[C:]
    forward(0)
    gate(1)
    prev_frame(0)
    for r in range(R):
        acc[0, r] += dot(w1[:C, :], window(0, r))
    gate(0)

    ow_up = copy(la.at[0], rxs.at[0], s_part.at[3], r_part.at[3], 0, -1)
    ow_dn = copy(la.at[R + 1], rxs.at[1], s_part.at[4], r_part.at[4], 0, 1)
    when(up_ok, ow_up.start)
    when(dn_ok, ow_dn.start)

    no = jnp.logical_not
    when(no(has_prev), zero(rxm, (slice(None),)))
    when(no(dn_ok), zero(rxs, (0,)))
    when(no(up_ok), zero(rxs, (1,)))
    when(no(both(has_prev, dn_ok)), zero(rxs, (2,)))
    when(no(both(has_prev, up_ok)), zero(rxs, (3,)))
    when(has_prev, nx_mid.wait_recv)
    when(both(has_prev, dn_ok), nx_up.wait_recv)
    when(both(has_prev, up_ok), nx_dn.wait_recv)
    when(dn_ok, ow_up.wait_recv)
    when(up_ok, ow_dn.wait_recv)
    for r in range(R):
        total = la[r + 1] + rxm[r]
        if r == 0:
            total = total + rxs[1] + rxs[3]
        if r == R - 1:
            total = total + rxs[0] + rxs[2]
        lr[3, r + 2] = total.astype(BF16)

    sends = []
    for d in range(4):
        for s in (0, -1, 1):
            if d == 0 and s == 0:
                continue
            src = {0: pl.ds(2, R), -1: pl.ds(2, 2), 1: pl.ds(R, 2)}[s]
            dst = {0: pl.ds(2, R), -1: pl.ds(R + 2, 2), 1: pl.ds(0, 2)}[s]
            c = copy(
                lr.at[3, src], lr.at[3 - d, dst], s_lat.at[d, s + 1], r_lat.at[d, s + 1], d, s
            )
            when(both(tm < spans - d if d else None, side_ok[s]), c.start)
            sends.append((d, s, c))
    lat_ref[...] = lr[3, 2 : R + 2]
    for d, s, c in sends:
        dst = {0: slice(2, R + 2), -1: slice(R + 2, R + 4), 1: slice(0, 2)}[s]
        ok = both(tm >= d if d else None, side_ok[-s])
        when(no(ok), zero(lr, (3 - d, dst)))
        when(ok, c.wait_recv)

    def lat_rows(row, _):
        for f in range(4):
            for e, part in enumerate(col_taps(lr[f, row].astype(F32))):
                ls[row, (f * 3 + e) * Z : (f * 3 + e + 1) * Z, :] = part
        return 0

    lax.fori_loop(0, R + 4, lat_rows, 0, unroll=True)
    bd = column(bd_ref)
    gd = column(gd_ref)
    prev_on = jnp.where(has_prev, 1.0, 0.0)

    def decode(row, _):
        k = jnp.concatenate([ls[row], ls[row + 1], ls[row + 2]], axis=0)
        y = dot(wd_ref[...], k)
        grow = rb * R + row - 1
        on = jnp.where(jnp.logical_and(grow >= 0, grow < bands * R), 1.0, 0.0)
        put_stack(act, 0, row, norm_silu(y[:C] + bd, gd) * (on * prev_on))
        put_stack(act, 1, row, norm_silu(y[C:] + bd, gd) * on)
        return 0

    lax.fori_loop(0, R + 2, decode, 0, unroll=True)

    def finish(r, _):
        cur = jnp.concatenate([act[1, r], act[1, r + 1], act[1, r + 2]], axis=0)
        old = jnp.concatenate([act[0, r], act[0, r + 1], act[0, r + 2]], axis=0)
        y = dot(w3[: 4 * C, :], cur)
        z = dot(w3[4 * C :, :], old)
        for j in range(4):
            part = y[j * C : (j + 1) * C]
            if j < 2:
                part = part + z[j * C : (j + 1) * C]
            out_ref[j, r] = part.astype(BF16)
        return 0

    lax.fori_loop(0, R, finish, 0, unroll=True)

    when(up_ok, own_up.wait_send)
    when(dn_ok, own_dn.wait_send)
    for c in ahead:
        when(has_next, c.wait_send)
    for f in range(2):
        when(both(has_prev, up_ok), fwd_up[f].wait_send)
        when(both(has_prev, dn_ok), fwd_dn[f].wait_send)
    when(has_next, nx_mid.wait_send)
    when(both(has_next, up_ok), nx_up.wait_send)
    when(both(has_next, dn_ok), nx_dn.wait_send)
    when(up_ok, ow_up.wait_send)
    when(dn_ok, ow_dn.wait_send)
    for d, s, c in sends:
        when(both(tm < spans - d if d else None, side_ok[s]), c.wait_send)


def body(
    spans,
    bands,
    features,
    first_kernel,
    first_bias,
    first_gain,
    second_kernel,
    latent_weight,
    decode_kernel,
    decode_bias,
    decode_gain,
    upsample_weight,
    final_kernel,
):
    T, C, R, W = features.shape
    Z = latent_weight.shape[1]
    x = features.transpose(0, 2, 1, 3)
    vmem = pl.BlockSpec(memory_space=pltpu.VMEM)
    lat, out = pl.pallas_call(
        functools.partial(kernel, spans, bands),
        out_shape=(
            jax.ShapeDtypeStruct((R, Z, W), BF16),
            jax.ShapeDtypeStruct((T, R, C, W), BF16),
        ),
        in_specs=[vmem] * 5 + [pl.BlockSpec(memory_space=pltpu.HBM)] * 6,
        out_specs=(vmem, vmem),
        scratch_shapes=[
            pltpu.VMEM((2, R, C, W), BF16),
            pltpu.VMEM((2, 6, C, W), BF16),
            pltpu.VMEM((6, R + 2, 3 * C, W), BF16),
            pltpu.VMEM((4, R, C, W), F32),
            pltpu.VMEM((3 * C, 9 * C), BF16),
            pltpu.VMEM((4, 6 * Z, 3 * C), BF16),
            pltpu.VMEM((6 * C, 9 * C), BF16),
            pltpu.VMEM((R + 2, Z, W), F32),
            pltpu.VMEM((R + 2, Z, W), F32),
            pltpu.VMEM((R, Z, W), F32),
            pltpu.VMEM((4, Z, W), F32),
            pltpu.VMEM((4, R + 4, Z, W), BF16),
            pltpu.VMEM((R + 4, 12 * Z, W), BF16),
            pltpu.VMEM((2, R + 2, 3 * C, W), BF16),
            pltpu.VMEM((27, C, C), BF16),
            pltpu.VMEM((27, C, C), BF16),
            pltpu.VMEM((4, Z, C), BF16),
            pltpu.VMEM((27, Z, C), BF16),
            pltpu.VMEM((4, C, C), BF16),
            pltpu.VMEM((27, C, C), BF16),
            pltpu.VMEM((2 * C, 36 * Z), BF16),
            pltpu.SemaphoreType.DMA((6,)),
            pltpu.SemaphoreType.DMA((12,)),
            pltpu.SemaphoreType.DMA((12,)),
            pltpu.SemaphoreType.DMA((5,)),
            pltpu.SemaphoreType.DMA((5,)),
            pltpu.SemaphoreType.DMA((4, 3)),
            pltpu.SemaphoreType.DMA((4, 3)),
        ],
        compiler_params=pltpu.CompilerParams(
            collective_id=0, has_side_effects=True, vmem_limit_bytes=48 * 1024 * 1024
        ),
    )(
        x,
        first_bias.reshape(1, C),
        first_gain.reshape(1, C),
        decode_bias.reshape(1, C),
        decode_gain.reshape(1, C),
        first_kernel.reshape(27, C, C),
        second_kernel.reshape(27, C, C),
        latent_weight,
        decode_kernel.transpose(0, 1, 2, 4, 3).reshape(27, Z, C),
        upsample_weight,
        final_kernel.reshape(27, C, C),
    )
    return lat.transpose(1, 0, 2)[None], out.transpose(0, 2, 1, 3)


def solution(mesh):
    spans = mesh.shape["tm"]
    bands = mesh.shape["rows"]
    return jax.shard_map(
        functools.partial(body, spans, bands),
        mesh=mesh,
        in_specs=(P("tm", None, "rows", None),) + (P(),) * 10,
        out_specs=(P("tm", None, "rows", None), P("tm", None, "rows", None)),
        check_vma=False,
    )
```

```python
import functools

import jax
import jax.numpy as jnp
from jax import lax
from jax.experimental import pallas as pl
from jax.experimental.pallas import tpu as pltpu
from jax.sharding import PartitionSpec as P

F32 = jnp.float32
BF16 = jnp.bfloat16
MESH = pl.DeviceIdType.MESH


def dot(a, b):
    return jnp.dot(a, b, preferred_element_type=F32)


def col_taps(x):
    w = x.shape[1]
    lane = lax.broadcasted_iota(jnp.int32, x.shape, 1)
    left = jnp.where(lane == 0, 0.0, pltpu.roll(x, 1, 1))
    right = jnp.where(lane == w - 1, 0.0, pltpu.roll(x, w - 1, 1))
    return left.astype(BF16), x.astype(BF16), right.astype(BF16)


def norm_silu(v, gain):
    scale = lax.rsqrt(jnp.mean(v * v, axis=0, keepdims=True) + 1e-6)
    u = v * scale * gain
    return u / (1.0 + jnp.exp(-u))


def kernel(
    spans,
    bands,
    x_ref,
    b1_ref,
    g1_ref,
    bd_ref,
    gd_ref,
    k1_ref,
    k2_ref,
    wl_ref,
    dk_ref,
    up_ref,
    k3_ref,
    lat_ref,
    out_ref,
    rx_t,
    rx_r,
    xs,
    acc,
    w1,
    v2,
    w3,
    la,
    ln,
    rxm,
    rxs,
    lr,
    ls,
    act,
    wd_ref,
    s_feat,
    r_feat,
    s_part,
    r_part,
    s_lat,
    r_lat,
):
    C = x_ref.shape[2]
    W = x_ref.shape[3]
    Z = wl_ref.shape[1]
    R = x_ref.shape[1]
    tm = lax.axis_index("tm")
    rb = lax.axis_index("rows")
    has_next = tm < spans - 1
    has_prev = tm > 0
    up_ok = rb > 0
    dn_ok = rb < bands - 1
    side_ok = {-1: up_ok, 0: None, 1: dn_ok}

    def both(*conds):
        out = None
        for c in conds:
            if c is None:
                continue
            out = c if out is None else jnp.logical_and(out, c)
        return out

    def when(cond, fn):
        if cond is None:
            fn()
        else:
            pl.when(cond)(fn)

    barrier = pltpu.get_barrier_semaphore()
    expect = jnp.int32(0)
    for d in range(4):
        for s in (-1, 0, 1):
            if (d == 0 and s == 0) or (d > 1 and s != 0):
                continue

            def greet(d=d, s=s):
                pl.semaphore_signal(
                    barrier, inc=1, device_id=(tm - d, rb + s), device_id_type=MESH
                )

            when(both(tm >= d, side_ok[s]) if d else side_ok[s], greet)
            ok = both(tm < spans - d, side_ok[s])
            expect = expect + jnp.where(ok, 1, 0)

    pl.semaphore_wait(barrier, expect)

    def copy(src, dst, ssem, rsem, d, s):
        return pltpu.make_async_remote_copy(
            src_ref=src,
            dst_ref=dst,
            send_sem=ssem,
            recv_sem=rsem,
            device_id=(tm + d, rb + s),
            device_id_type=MESH,
        )

    own_up = copy(x_ref.at[:, 0], rx_r.at[1, pl.ds(2, 4)], s_feat.at[0], r_feat.at[0], 0, -1)
    own_dn = copy(x_ref.at[:, R - 1], rx_r.at[0, pl.ds(2, 4)], s_feat.at[1], r_feat.at[1], 0, 1)
    pieces = [(1, 0, 1), (1, R - 1, 1), (1, 1, R - 2), (0, 0, 1), (0, R - 1, 1), (0, 1, R - 2)]
    ahead = [
        copy(
            x_ref.at[2 + f, pl.ds(r, n)],
            rx_t.at[f, pl.ds(r, n)],
            s_feat.at[2 + i],
            r_feat.at[2 + i],
            1,
            0,
        )
        for i, (f, r, n) in enumerate(pieces)
    ]
    fwd_up = [
        copy(rx_t.at[f, 0], rx_r.at[1, f], s_feat.at[8 + f], r_feat.at[8 + f], 0, -1)
        for f in range(2)
    ]
    fwd_dn = [
        copy(rx_t.at[f, R - 1], rx_r.at[0, f], s_feat.at[10 + f], r_feat.at[10 + f], 0, 1)
        for f in range(2)
    ]
    for c in ahead:
        when(has_next, c.start)
    when(up_ok, own_up.start)
    when(dn_ok, own_dn.start)

    def zero(ref, idx):
        def go():
            ref[idx] = jnp.zeros(ref[idx].shape, ref.dtype)

        return go

    when(jnp.logical_not(up_ok), zero(rx_r, (0,)))
    when(jnp.logical_not(dn_ok), zero(rx_r, (1,)))

    def column(ref):
        c = ref.shape[1]
        i = lax.broadcasted_iota(jnp.int32, (c, c), 0)
        j = lax.broadcasted_iota(jnp.int32, (c, c), 1)
        return jnp.sum(jnp.where(i == j, ref[...], 0.0), axis=1, keepdims=True)

    for a in range(3):
        w1[a * C : (a + 1) * C, :] = jnp.concatenate(
            [k1_ref[a * 9 + be] for be in range(9)], axis=1
        )

    def put_stack(ref, f, row, x):
        for e, part in enumerate(col_taps(x)):
            ref[f, row, e * C : (e + 1) * C, :] = part

    def own_rows(i, _):
        f, r = i // R, i % R
        put_stack(xs, f + 2, r + 1, x_ref[f, r].astype(F32))
        return 0

    lax.fori_loop(0, 4 * R, own_rows, 0, unroll=True)

    wl = jnp.concatenate([wl_ref[j] for j in range(4)], axis=0)
    for b in range(3):
        g = [[dot(wl, k2_ref[a * 9 + b * 3 + e]) for e in range(3)] for a in range(3)]
        for f in range(4):
            rows = []
            own = [(j, f - j + 2) for j in range(4) if 0 <= f - j + 2 <= 2]
            nxt = [(j, f - 2 - j) for j in range(4) if 0 <= f - 2 - j <= 2]
            for terms in (own, nxt):
                if not terms:
                    continue
                rows.append(
                    jnp.concatenate(
                        [sum(g[a][e][j * Z : (j + 1) * Z] for j, a in terms) for e in range(3)],
                        axis=1,
                    ).astype(BF16)
                )
            n = len(rows)
            for i in range(n):
                v2[f, (b * n + i) * Z : (b * n + i + 1) * Z, :] = rows[i]

    when(dn_ok, own_up.wait_recv)
    when(up_ok, own_dn.wait_recv)

    def halo_rows(first):
        def go(f, _):
            put_stack(xs, f, 0, rx_r[0, f].astype(F32))
            put_stack(xs, f, R + 1, rx_r[1, f].astype(F32))
            return 0

        return go

    lax.fori_loop(2, 6, halo_rows(2), 0, unroll=True)
    b1 = column(b1_ref)
    g1 = column(g1_ref)

    def window(f, r):
        return jnp.concatenate([xs[f, r], xs[f, r + 1], xs[f, r + 2]], axis=0)

    def conv_own(r, _):
        for fi in range(2, 6):
            lo, hi = max(0, fi - 3), min(2, fi)
            y = dot(w1[lo * C : (hi + 1) * C, :], window(fi, r))
            for a in range(lo, hi + 1):
                t = fi - a
                part = y[(a - lo) * C : (a - lo + 1) * C]
                if (fi == 2) or (fi == 3 and t == 3):
                    acc[t, r] = part + b1
                else:
                    acc[t, r] += part
        return 0

    lax.fori_loop(0, R, conv_own, 0, unroll=True)

    la[...] = jnp.zeros(la.shape, F32)
    ln[...] = jnp.zeros(ln.shape, F32)

    def gate(t):
        def go(r, _):
            gated = norm_silu(acc[t, r], g1)
            stack = jnp.concatenate(col_taps(gated), axis=0)
            n = 2 if t >= 2 else 1
            y = dot(v2[t, : 3 * n * Z, :], stack)
            for b in range(3):
                la[r - b + 2] += y[b * n * Z : (b * n + 1) * Z]
                if n == 2:
                    ln[r - b + 2] += y[(b * n + 1) * Z : (b * n + 2) * Z]
            la[r + 1] += dot(wl_ref[t], x_ref[t, r])
            return 0

        lax.fori_loop(0, R, go, 0, unroll=True)

    gate(2)
    gate(3)

    nx_mid = copy(ln.at[pl.ds(1, R)], rxm, s_part.at[0], r_part.at[0], 1, 0)
    nx_up = copy(ln.at[0], rxs.at[2], s_part.at[1], r_part.at[1], 1, -1)
    nx_dn = copy(ln.at[R + 1], rxs.at[3], s_part.at[2], r_part.at[2], 1, 1)
    when(has_next, nx_mid.start)
    when(both(has_next, up_ok), nx_up.start)
    when(both(has_next, dn_ok), nx_dn.start)

    def no_prev():
        rx_t[...] = jnp.zeros(rx_t.shape, BF16)
        rx_r[0, 0:2] = jnp.zeros((2, C, W), BF16)
        rx_r[1, 0:2] = jnp.zeros((2, C, W), BF16)

    when(jnp.logical_not(has_prev), no_prev)

    def forward(f):
        base = 0 if f == 1 else 3
        when(has_prev, ahead[base].wait_recv)
        when(both(has_prev, up_ok), fwd_up[f].start)
        when(has_prev, ahead[base + 1].wait_recv)
        when(both(has_prev, dn_ok), fwd_dn[f].start)

    forward(1)
    taps = []
    for b in range(3):
        for f in range(4):
            for e in range(3):
                taps.append((f, b * 3 + e))
    none = jnp.zeros((Z, C), BF16)
    wd_ref[:C, :] = jnp.transpose(
        jnp.concatenate([dk_ref[f * 9 + be] if f < 3 else none for f, be in taps], axis=0)
    )
    wd_ref[C:, :] = jnp.transpose(
        jnp.concatenate([dk_ref[(f - 1) * 9 + be] if f > 0 else none for f, be in taps], axis=0)
    )

    ups = [up_ref[j] for j in range(4)]
    for be in range(9):
        k3 = jnp.concatenate([k3_ref[a * 9 + be] for a in range(3)], axis=0)
        f3 = [dot(k3, ups[j]) for j in range(4)]
        for j in range(4):
            total = sum(f3[j + a - 2][a * C : (a + 1) * C] for a in range(3) if j + a >= 2)
            if be == 4:
                total = total + ups[j].astype(F32)
            w3[j * C : (j + 1) * C, be * C : (be + 1) * C] = total.astype(BF16)
        for j in range(2):
            total = sum(f3[j + a + 2][a * C : (a + 1) * C] for a in range(3) if j + a < 2)
            w3[(4 + j) * C : (5 + j) * C, be * C : (be + 1) * C] = total.astype(BF16)

    def prev_frame(f):
        when(has_prev, ahead[2 if f == 1 else 5].wait_recv)
        for r in range(R):
            put_stack(xs, f, r + 1, rx_t[f, r].astype(F32))
        when(both(has_prev, dn_ok), fwd_up[f].wait_recv)
        when(both(has_prev, up_ok), fwd_dn[f].wait_recv)
        put_stack(xs, f, 0, rx_r[0, f].astype(F32))
        put_stack(xs, f, R + 1, rx_r[1, f].astype(F32))

    prev_frame(1)
    for r in range(R):
        y = dot(w1[: 2 * C, :], window(1, r))
        acc[1, r] += y[:C]
        acc[0, r] += y[C:]
    forward(0)
    gate(1)
    prev_frame(0)
    for r in range(R):
        acc[0, r] += dot(w1[:C, :], window(0, r))
    gate(0)

    ow_up = copy(la.at[0], rxs.at[0], s_part.at[3], r_part.at[3], 0, -1)
    ow_dn = copy(la.at[R + 1], rxs.at[1], s_part.at[4], r_part.at[4], 0, 1)
    when(up_ok, ow_up.start)
    when(dn_ok, ow_dn.start)

    no = jnp.logical_not
    when(no(has_prev), zero(rxm, (slice(None),)))
    when(no(dn_ok), zero(rxs, (0,)))
    when(no(up_ok), zero(rxs, (1,)))
    when(no(both(has_prev, dn_ok)), zero(rxs, (2,)))
    when(no(both(has_prev, up_ok)), zero(rxs, (3,)))
    when(has_prev, nx_mid.wait_recv)
    when(both(has_prev, dn_ok), nx_up.wait_recv)
    when(both(has_prev, up_ok), nx_dn.wait_recv)
    when(dn_ok, ow_up.wait_recv)
    when(up_ok, ow_dn.wait_recv)
    for r in range(R):
        total = la[r + 1] + rxm[r]
        if r == 0:
            total = total + rxs[1] + rxs[3]
        if r == R - 1:
            total = total + rxs[0] + rxs[2]
        lr[3, r + 2] = total.astype(BF16)

    sends = [
        (
            copy(
                lr.at[3, pl.ds(2, R)],
                lr.at[3 - d, pl.ds(2, R)],
                s_lat.at[d, 1],
                r_lat.at[d, 1],
                d,
                0,
            ),
            tm < spans - d,
            tm >= d,
            (3 - d, slice(2, R + 2)),
        )
        for d in (1, 2, 3)
    ]
    for c, there, _, _ in sends:
        when(there, c.start)

    def side(f, s):
        src, dst = (2, R + 2) if s < 0 else (R, 0)
        return copy(
            lr.at[f, pl.ds(src, 2)],
            lr.at[f, pl.ds(dst, 2)],
            s_lat.at[3 - f, s + 1],
            r_lat.at[3 - f, s + 1],
            0,
            s,
        )

    sides = [[side(f, s) for s in (-1, 1)] for f in range(4)]
    when(up_ok, sides[3][0].start)
    when(dn_ok, sides[3][1].start)
    lat_ref[...] = lr[3, 2 : R + 2]
    for c, _, here, where in sends:
        when(no(here), zero(lr, where))
        when(here, c.wait_recv)
        f = where[0]
        when(both(here, up_ok), sides[f][0].start)
        when(both(here, dn_ok), sides[f][1].start)
    for f in (3, 2, 1, 0):
        here = None if f == 3 else tm >= 3 - f
        for ok, c, where in (
            (both(here, dn_ok), sides[f][0], slice(R + 2, R + 4)),
            (both(here, up_ok), sides[f][1], slice(0, 2)),
        ):
            when(no(ok), zero(lr, (f, where)))
            when(ok, c.wait_recv)

    def lat_rows(row, _):
        for f in range(4):
            for e, part in enumerate(col_taps(lr[f, row].astype(F32))):
                ls[row, (f * 3 + e) * Z : (f * 3 + e + 1) * Z, :] = part
        return 0

    lax.fori_loop(0, R + 4, lat_rows, 0, unroll=True)
    bd = column(bd_ref)
    gd = column(gd_ref)
    prev_on = jnp.where(has_prev, 1.0, 0.0)

    def decode(row, _):
        k = jnp.concatenate([ls[row], ls[row + 1], ls[row + 2]], axis=0)
        y = dot(wd_ref[...], k)
        grow = rb * R + row - 1
        on = jnp.where(jnp.logical_and(grow >= 0, grow < bands * R), 1.0, 0.0)
        put_stack(act, 0, row, norm_silu(y[:C] + bd, gd) * (on * prev_on))
        put_stack(act, 1, row, norm_silu(y[C:] + bd, gd) * on)
        return 0

    lax.fori_loop(0, R + 2, decode, 0, unroll=True)

    def finish(r, _):
        cur = jnp.concatenate([act[1, r], act[1, r + 1], act[1, r + 2]], axis=0)
        old = jnp.concatenate([act[0, r], act[0, r + 1], act[0, r + 2]], axis=0)
        y = dot(w3[: 4 * C, :], cur)
        z = dot(w3[4 * C :, :], old)
        for j in range(4):
            part = y[j * C : (j + 1) * C]
            if j < 2:
                part = part + z[j * C : (j + 1) * C]
            out_ref[j, r] = part.astype(BF16)
        return 0

    lax.fori_loop(0, R, finish, 0, unroll=True)

    when(up_ok, own_up.wait_send)
    when(dn_ok, own_dn.wait_send)
    for c in ahead:
        when(has_next, c.wait_send)
    for f in range(2):
        when(both(has_prev, up_ok), fwd_up[f].wait_send)
        when(both(has_prev, dn_ok), fwd_dn[f].wait_send)
    when(has_next, nx_mid.wait_send)
    when(both(has_next, up_ok), nx_up.wait_send)
    when(both(has_next, dn_ok), nx_dn.wait_send)
    when(up_ok, ow_up.wait_send)
    when(dn_ok, ow_dn.wait_send)
    for c, there, _, _ in sends:
        when(there, c.wait_send)
    for f in range(4):
        here = None if f == 3 else tm >= 3 - f
        when(both(here, up_ok), sides[f][0].wait_send)
        when(both(here, dn_ok), sides[f][1].wait_send)


def body(
    spans,
    bands,
    features,
    first_kernel,
    first_bias,
    first_gain,
    second_kernel,
    latent_weight,
    decode_kernel,
    decode_bias,
    decode_gain,
    upsample_weight,
    final_kernel,
):
    T, C, R, W = features.shape
    Z = latent_weight.shape[1]
    x = features.transpose(0, 2, 1, 3)
    vmem = pl.BlockSpec(memory_space=pltpu.VMEM)
    lat, out = pl.pallas_call(
        functools.partial(kernel, spans, bands),
        out_shape=(
            jax.ShapeDtypeStruct((R, Z, W), BF16),
            jax.ShapeDtypeStruct((T, R, C, W), BF16),
        ),
        in_specs=[vmem] * 11,
        out_specs=(vmem, vmem),
        scratch_shapes=[
            pltpu.VMEM((2, R, C, W), BF16),
            pltpu.VMEM((2, 6, C, W), BF16),
            pltpu.VMEM((6, R + 2, 3 * C, W), BF16),
            pltpu.VMEM((4, R, C, W), F32),
            pltpu.VMEM((3 * C, 9 * C), BF16),
            pltpu.VMEM((4, 6 * Z, 3 * C), BF16),
            pltpu.VMEM((6 * C, 9 * C), BF16),
            pltpu.VMEM((R + 2, Z, W), F32),
            pltpu.VMEM((R + 2, Z, W), F32),
            pltpu.VMEM((R, Z, W), F32),
            pltpu.VMEM((4, Z, W), F32),
            pltpu.VMEM((4, R + 4, Z, W), BF16),
            pltpu.VMEM((R + 4, 12 * Z, W), BF16),
            pltpu.VMEM((2, R + 2, 3 * C, W), BF16),
            pltpu.VMEM((2 * C, 36 * Z), BF16),
            pltpu.SemaphoreType.DMA((12,)),
            pltpu.SemaphoreType.DMA((12,)),
            pltpu.SemaphoreType.DMA((5,)),
            pltpu.SemaphoreType.DMA((5,)),
            pltpu.SemaphoreType.DMA((4, 3)),
            pltpu.SemaphoreType.DMA((4, 3)),
        ],
        compiler_params=pltpu.CompilerParams(
            collective_id=0, has_side_effects=True, vmem_limit_bytes=24 * 1024 * 1024
        ),
    )(
        x,
        first_bias.reshape(1, C),
        first_gain.reshape(1, C),
        decode_bias.reshape(1, C),
        decode_gain.reshape(1, C),
        first_kernel.reshape(27, C, C),
        second_kernel.reshape(27, C, C),
        latent_weight,
        decode_kernel.transpose(0, 1, 2, 4, 3).reshape(27, Z, C),
        upsample_weight,
        final_kernel.reshape(27, C, C),
    )
    return lat.transpose(1, 0, 2)[None], out.transpose(0, 2, 1, 3)


def solution(mesh):
    spans = mesh.shape["tm"]
    bands = mesh.shape["rows"]
    return jax.shard_map(
        functools.partial(body, spans, bands),
        mesh=mesh,
        in_specs=(P("tm", None, "rows", None),) + (P(),) * 10,
        out_specs=(P("tm", None, "rows", None), P("tm", None, "rows", None)),
        check_vma=False,
    )
```
